512 devices in a mesh: head: 8 (over z_hi, core), batch: 64 (over y, x, z_lo).
Axes of the slice: x: 4, y: 4, z: 16 (z_hi: 4, z_lo: 4; z = z_hi * 4 + z_lo), core: 2. Of those that a mesh axis runs over, the one named last changes fastest.
Arguments:
- prompt_kv: bfloat16 [64, 1024, 2048], P(None, ('head', 'batch')), may hold values from -6 to 6
- prompt_lengths: int32 [64], replicated, may hold values from 128 to 1024, as said below
- owner_prompts: int32 [64, 2], replicated, may hold values from 0 to 63, as said below
- owner_counts: int32 [64], P('batch'), may hold values from 0 to 32, as said below
- queries: bfloat16 [2048, 4, 8192], P('batch', None, 'head'), may hold values from -40 to 40
- new_kv: bfloat16 [2048, 4, 2048], P('batch', None, 'head'), may hold values from -6 to 6
Outputs:
- attention: bfloat16 [2048, 4, 8192], P('batch', None, 'head')
The draws below stay inside these ranges and needn't reach their ends.
Inputs may be any that keep to these rules, and one draw needn't show every extreme that they name: `prompt_lengths`: some prompt has each end of the range as its length. `owner_prompts`: the first owner_counts[o] / 16 entries of row o are live and, over all rows, the live entries name every prompt exactly once; other entries are arbitrary prompt ids. `owner_counts`: multiples of 16 that sum to 1024; some owner holds 32 samples.
All inputs are finite; a program needn't handle non-finite values.
Results may differ from the reference program's by a relative error of at most 0.003.
Values may be sent and summed in bfloat16 or wider, within the bound.
A program may use at most 64 MiB of HBM per device.

```python
import math
import jax
import jax.numpy as jnp
from jax import lax

HD = 128
QH = 64
KVH = 8
GROUP = 16
STEPS = 4
PSLOTS = 2
PROMPTS = 64
MAXLEN = 1024
SLOTS = 32
N_BATCH = 64


def owner_plan(key):
    key = jax.random.fold_in(key, 5)
    first_key, shift_key, order_key, spare_key = jax.random.split(key, 4)
    pair_count = N_BATCH // 2
    first = jax.random.randint(first_key, (pair_count,), 0, PSLOTS + 1)
    first = first.at[0].set(PSLOTS)
    groups = jnp.stack([first, PSLOTS - first], axis=1).reshape(N_BATCH)
    shift = jax.random.randint(shift_key, (), 0, N_BATCH)
    groups = groups[(jnp.arange(N_BATCH) - shift) % N_BATCH]
    starts = jnp.cumsum(groups) - groups
    order = jax.random.permutation(order_key, PROMPTS)
    slot_rank = jnp.arange(PSLOTS)[None, :]
    live = slot_rank < groups[:, None]
    picked = order[jnp.clip(starts[:, None] + slot_rank, 0, PROMPTS - 1)]
    spare = jax.random.randint(spare_key, (N_BATCH, PSLOTS), 0, PROMPTS)
    lists = jnp.where(live, picked, spare)
    return (lists.astype(jnp.int32), (groups * GROUP).astype(jnp.int32))


def draw_owner_prompts(key, part):
    return owner_plan(key)[0]


def draw_owner_counts(key, part):
    return owner_plan(key)[1]


def draw_prompt_lengths(key, part):
    key = jax.random.fold_in(key, 17)
    first_key, long_key, short_key = jax.random.split(key, 3)
    lowest = MAXLEN // 8
    lengths = jax.random.randint(first_key, (PROMPTS,), lowest, MAXLEN + 1)
    longest = jax.random.randint(long_key, (), 0, PROMPTS)
    shortest = (longest + 1 + jax.random.randint(short_key, (), 0, PROMPTS - 1)) % PROMPTS
    lengths = lengths.at[longest].set(MAXLEN).at[shortest].set(lowest)
    return lengths.astype(jnp.int32)


def draw_queries(key, part):
    key = jax.random.fold_in(key, 23)
    base_key = jax.random.fold_in(key, 0)
    shape = (N_BATCH * SLOTS, STEPS, KVH, QH // KVH, HD)
    values = 2.5 * jnp.clip(jax.random.normal(base_key, shape, jnp.float32), -4.0, 4.0)
    return values.reshape(N_BATCH * SLOTS, STEPS, QH * HD).astype(jnp.bfloat16)


def draw_prompt_kv(key, part):
    key = jax.random.fold_in(key, 31)
    shape = (PROMPTS, MAXLEN, KVH, 2, HD)
    values = jnp.clip(jax.random.normal(key, shape, jnp.float32), -6.0, 6.0)
    return values.reshape(PROMPTS, MAXLEN, 2 * KVH * HD).astype(jnp.bfloat16)


def steps_of(key, extent, pieces, low, largest):
    def one(dim, parts):
        draws = jax.random.uniform(jax.random.fold_in(jax.random.fold_in(key, 6), dim), (parts,), jnp.float32, low / len(pieces), largest / len(pieces))
        return jnp.repeat(jnp.exp(draws), extent[dim] // parts).reshape((-1,) + (1,) * (len(extent) - dim - 1))

    gain = one(*pieces[0])
    for cut in pieces[1:]:
        gain = gain * one(*cut)
    return gain


def centred(rng, dims, scale, limit, cuts=(), kind=jnp.bfloat16):
    entries = jax.random.normal(rng, dims, jnp.float32) * scale
    if len(cuts) > 0:
        entries = steps_of(rng, dims, cuts, -0.22, 0.18) * entries
    return jnp.clip(entries, min=-limit, max=limit).astype(kind)


def setup_inputs(seed: int = 0) -> dict:
    seeds = jax.random.split(jax.random.key(seed), 7)
    prompt_kv = draw_prompt_kv(jax.random.fold_in(seeds[6], 71), 0)
    prompt_lengths = draw_prompt_lengths(jax.random.fold_in(seeds[6], 71), 0)
    owner_prompts = draw_owner_prompts(jax.random.fold_in(seeds[6], 71), 0)
    owner_counts = draw_owner_counts(jax.random.fold_in(seeds[6], 71), 0)
    queries = draw_queries(jax.random.fold_in(seeds[6], 71), 0)
    new_kv = centred(seeds[5], (N_BATCH * SLOTS, STEPS, 2 * KVH * HD), 1.0, 6.0, ((0, 64), (2, 8)))
    return dict(prompt_kv=prompt_kv, prompt_lengths=prompt_lengths, owner_prompts=owner_prompts, owner_counts=owner_counts, queries=queries, new_kv=new_kv)


def reference(prompt_kv, prompt_lengths, owner_prompts, owner_counts, queries, new_kv):
    per_kv = QH // KVH
    scale = 1.0 / math.sqrt(HD)
    items = N_BATCH * PSLOTS
    flat_query = queries.reshape(items, GROUP, STEPS, KVH, per_kv, HD)
    flat_own = new_kv.reshape(items, GROUP, STEPS, KVH, 2, HD)
    flat_prompt = owner_prompts.reshape(items).astype(jnp.int32)
    slot_first = jnp.arange(items, dtype=jnp.int32) % PSLOTS * GROUP
    counts_each = jnp.repeat(owner_counts.astype(jnp.int32), PSLOTS)
    causal = jnp.arange(STEPS, dtype=jnp.int32)[None, :] <= jnp.arange(STEPS, dtype=jnp.int32)[:, None]
    highest = lax.Precision.HIGHEST

    def attend(item):
        query_rows, own_rows, prompt_id, first_slot, count = item
        query_f = query_rows.astype(jnp.float32)
        own_f = own_rows.astype(jnp.float32)
        cache = lax.dynamic_index_in_dim(prompt_kv, prompt_id, 0, keepdims=False)
        cache = cache.reshape(MAXLEN, KVH, 2, HD).astype(jnp.float32)
        length = lax.dynamic_index_in_dim(prompt_lengths, prompt_id, 0, keepdims=False)
        prompt_scores = jnp.einsum('gtjqd,njd->gtjqn', query_f, cache[:, :, 0, :], precision=highest) * scale
        valid = jnp.arange(MAXLEN, dtype=jnp.int32) < length
        prompt_scores = jnp.where(valid, prompt_scores, -jnp.inf)
        own_scores = jnp.einsum('gtjqd,gujd->gtjqu', query_f, own_f[:, :, :, 0, :], precision=highest) * scale
        own_scores = jnp.where(causal[None, :, None, None, :], own_scores, -jnp.inf)
        top = jnp.maximum(lax.optimization_barrier(jnp.max(prompt_scores, axis=-1)), lax.optimization_barrier(jnp.max(own_scores, axis=-1)))
        prompt_exps = jnp.exp(prompt_scores - top[..., None])
        own_exps = jnp.exp(own_scores - top[..., None])
        denominator = lax.optimization_barrier(jnp.sum(prompt_exps, axis=-1)) + lax.optimization_barrier(jnp.sum(own_exps, axis=-1))
        prompt_weights = lax.optimization_barrier(prompt_exps.astype(jnp.bfloat16)).astype(jnp.float32)
        own_weights = lax.optimization_barrier(own_exps.astype(jnp.bfloat16)).astype(jnp.float32)
        summed = jnp.einsum('gtjqn,njd->gtjqd', prompt_weights, cache[:, :, 1, :], precision=highest)
        summed = summed + jnp.einsum('gtjqu,gujd->gtjqd', own_weights, own_f[:, :, :, 1, :], precision=highest)
        mixed = summed / denominator[..., None]
        live = first_slot + jnp.arange(GROUP, dtype=jnp.int32) < count
        return jnp.where(live[:, None, None, None, None], mixed, 0.0).astype(jnp.bfloat16)
    outcome = lax.map(attend, (flat_query, flat_own, flat_prompt, slot_first, counts_each))
    return outcome.reshape(N_BATCH * SLOTS, STEPS, QH * HD)
```

```python
import math

import jax
import jax.numpy as jnp
from jax import lax
from jax.experimental import pallas as pl
from jax.experimental.pallas import tpu as pltpu
from jax.sharding import PartitionSpec as P

HD = 128
GROUP = 16
STEPS = 4
PER_KV = 8
HEADS = 8
PROMPTS = 64
SLOTS = 2
OWNERS = 64
RUNS = 4
POS = 2
MESH = pl.DeviceIdType.MESH
LOWEST = -1e30
SCALE = math.log2(math.e) / math.sqrt(HD)


def iota(shape, dim):
    return lax.broadcasted_iota(jnp.int32, shape, dim)


def place():
    head, batch = lax.axis_index("head"), lax.axis_index("batch")
    return head // 2, head % 2, batch // 4, batch % 4


def device(run, core, yx, node):
    return (lax.rem(run + RUNS, RUNS) * 2 + core, yx * 4 + node)


def relay_of(hop):
    run, _, _, node = place()
    odd, upper = node % 2, node // 2 == 1
    if hop == 1:
        return jnp.where(upper, run + 1, run + 3), jnp.where(upper, odd, 2 + odd)
    if hop == 2:
        return jnp.where(upper, run + 3, run + 1), jnp.where(upper, 2 + odd, odd)
    return run + 2, jnp.where(upper, odd, 2 + odd)


def source_of(hop, run, node):
    odd, upper = node % 2, node // 2 == 1
    if hop == 0:
        return run + 0 * node, node
    if hop == 1:
        return jnp.where(upper, run + 1, run + 3), jnp.where(upper, odd, 2 + odd)
    if hop == 2:
        return jnp.where(upper, run + 1, run + 3), jnp.where(upper, 2 + odd, odd)
    return run + 2, jnp.where(upper, odd, 2 + odd)


def kernel(lengths, prompts, counts, prompts_v, kv_hbm, q_hbm, new_hbm, out_ref,
           kv, q, new, wide, send, land, picked, got, pick, sort, qt, top, total, acc,
           in_sem, s1, r1, s2, r2):
    run, core, yx, node = place()
    me_head, me = lax.axis_index("head"), lax.axis_index("batch")

    loads = [pltpu.make_async_copy(a, b, in_sem.at[i]) for i, (a, b) in enumerate(((kv_hbm, kv), (q_hbm, q), (new_hbm, new)))]
    for load in loads:
        load.start()

    barrier = pltpu.get_barrier_semaphore()
    for hop in (3, 2, 1):
        their_run, their_node = source_of(hop, run, node)
        for k in (0, 1):
            pl.semaphore_signal(barrier, inc=1, device_id=device(their_run, k, yx, their_node), device_id_type=MESH)
    pl.semaphore_signal(barrier, inc=1, device_id=device(run, 1 - core, yx, node), device_id_type=MESH)

    @pl.loop(1, OWNERS)
    def _(i):
        pl.semaphore_signal(barrier, inc=1, device_id=(me_head, lax.rem(me + i, OWNERS)), device_id_type=MESH)

    loads[0].wait()
    for p in range(PROMPTS):
        wide[POS * p : POS * (p + 1), :] = kv[p].astype(jnp.float32)
    for h in range(HEADS):
        send[h] = wide[:, h * 256 : (h + 1) * 256].astype(jnp.bfloat16)

    rows, cols = OWNERS * 8, 2 * PROMPTS * POS
    owner_hot = (iota((rows, OWNERS), 0) // 8 == iota((rows, OWNERS), 1)).astype(jnp.bfloat16)
    ids = jnp.dot(owner_hot, prompts_v[...].astype(jnp.float32).astype(jnp.bfloat16), preferred_element_type=jnp.float32)
    r1d = iota((rows, 1), 0)
    ids = jnp.where(r1d // 4 % 2 == 0, ids[:, 0:1], ids[:, 1:2]).astype(jnp.int32)
    want = (r1d // 2 % 2) * (PROMPTS * POS) + ids * POS + r1d % 2
    pick[...] = (want == iota((rows, cols), 1)).astype(jnp.bfloat16)

    pl.semaphore_wait(barrier, 7 + OWNERS - 1)

    own = pltpu.make_async_copy(send.at[me_head], land.at[0, core], r1.at[0])
    own.start()
    first = []
    first.append(pltpu.make_async_remote_copy(
        send.at[run * 2 + 1 - core], land.at[0, core], s1.at[0], r1.at[0],
        device_id=device(run, 1 - core, yx, node), device_id_type=MESH))
    for hop in (1, 2, 3):
        to_run, to_node = relay_of(hop)
        for k in (0, 1):
            to = device(to_run, k, yx, to_node)
            first.append(pltpu.make_async_remote_copy(
                send.at[to[0]], land.at[hop, core], s1.at[2 * hop - 1 + k], r1.at[hop], device_id=to, device_id_type=MESH))
    for copy in first:
        copy.start()

    def relay(g):
        pltpu.make_async_copy(land.at[g], land.at[g], r1.at[g]).wait()
        found = jnp.dot(pick[...], land[g].reshape(cols, 256), preferred_element_type=jnp.float32)
        keys, values = found[:, :HD].reshape(OWNERS, 8, HD), found[:, HD:].reshape(OWNERS, 8, HD)
        picked[g] = jnp.concatenate([keys, values], axis=1).astype(jnp.bfloat16)
        pltpu.make_async_copy(picked.at[g, me], got.at[g, me], r2.at[g]).start()

        @pl.loop(1, OWNERS)
        def _(i):
            to = lax.rem(me + i, OWNERS)
            pltpu.make_async_remote_copy(
                picked.at[g, to], got.at[g, me], s2.at[g], r2.at[g],
                device_id=(me_head, to), device_id_type=MESH).start()

    relay(0)

    loads[1].wait()
    loads[2].wait()
    for g in range(GROUP * SLOTS):
        wide[STEPS * g : STEPS * (g + 1), :1024] = q[g].astype(jnp.float32)
        wide[STEPS * g : STEPS * (g + 1), 1024:1280] = new[g].astype(jnp.float32)
    side = 64
    rows = PER_KV * side
    for s in range(SLOTS):
        part = wide[side * s : side * (s + 1), :1024].astype(jnp.bfloat16)
        flat = jnp.concatenate([part[:, i * HD : (i + 1) * HD] for i in range(PER_KV)], axis=0)
        qt[s] = flat.astype(jnp.float32).T.astype(jnp.bfloat16)
        mine = wide[side * s : side * (s + 1), 1024:1280].astype(jnp.bfloat16)
        scores = jnp.dot(mine[:, :HD], qt[s], preferred_element_type=jnp.float32) * SCALE
        key, query = iota((side, rows), 0), iota((side, rows), 1) % side
        seen = (key // STEPS == query // STEPS) & (key % STEPS <= query % STEPS)
        scores = jnp.where(seen, scores, LOWEST)
        m = jnp.max(scores, axis=0, keepdims=True)
        e = jnp.where(seen, jnp.exp2(scores - m), 0.0)
        top[s : s + 1, :] = m
        total[s : s + 1, :] = jnp.sum(e, axis=0, keepdims=True)
        acc[s] = lax.dot_general(mine[:, HD:], e.astype(jnp.bfloat16), (((0,), (0,)), ((), ())), preferred_element_type=jnp.float32)

    r, c = iota((256, 256), 0), iota((256, 256), 1)
    sort[...] = (c == (r // 4 % 16) * 16 + (r // 64) * 4 + r % 4).astype(jnp.bfloat16)

    relay(1)
    relay(2)
    relay(3)

    def attend(g):
        pltpu.make_async_copy(got.at[g], got.at[g], r2.at[g]).wait()
        flat = got[g].reshape(OWNERS * 16, HD)
        blocks = [
            jnp.dot(sort[...], flat[256 * i : 256 * (i + 1)], preferred_element_type=jnp.float32).astype(jnp.bfloat16)
            for i in range(4)
        ]
        n = iota((256, rows), 0)
        relay_id = n // 4
        from_run, from_node = source_of(g, run, relay_id % 4)
        from_head = lax.rem(from_run + RUNS, RUNS) * 2 + n // 2 % 2
        position = (from_head * OWNERS + relay_id // 4 * 4 + from_node) * POS + n % 2
        for s in range(SLOTS):
            keys = jnp.concatenate([b[64 * s : 64 * (s + 1)] for b in blocks], axis=0)
            values = jnp.concatenate([b[128 + 64 * s : 128 + 64 * (s + 1)] for b in blocks], axis=0)
            scores = jnp.dot(keys, qt[s], preferred_element_type=jnp.float32) * SCALE
            scores = jnp.where(position < lengths[prompts[me, s]], scores, LOWEST)
            before = top[s : s + 1, :]
            m = jnp.maximum(before, jnp.max(scores, axis=0, keepdims=True))
            e = jnp.exp2(scores - m)
            fade = jnp.exp2(before - m)
            top[s : s + 1, :] = m
            total[s : s + 1, :] = total[s : s + 1, :] * fade + jnp.sum(e, axis=0, keepdims=True)
            acc[s] = acc[s] * fade + lax.dot_general(
                values, e.astype(jnp.bfloat16), (((0,), (0,)), ((), ())), preferred_element_type=jnp.float32)

    for g in range(4):
        attend(g)

    for s in range(SLOTS):
        live = s * GROUP < counts[0]
        result = jnp.where(live, acc[s] / total[s : s + 1, :], 0.0).T.astype(jnp.bfloat16)
        for i in range(PER_KV):
            out_ref[side * s : side * (s + 1), i * HD : (i + 1) * HD] = result[side * i : side * (i + 1)]

    for copy in first:
        copy.wait_send()
    for g in range(4):
        sent = picked.at[g, pl.ds(0, OWNERS - 1)]
        pltpu.make_async_copy(sent, sent, s2.at[g]).wait()


def local(prompt_kv, prompt_lengths, owner_prompts, owner_counts, queries, new_kv):
    smem, any_space = pl.BlockSpec(memory_space=pltpu.SMEM), pl.BlockSpec(memory_space=pl.ANY)
    vmem = pl.BlockSpec(memory_space=pltpu.VMEM)
    bf16, f32 = jnp.bfloat16, jnp.float32
    result = pl.pallas_call(
        kernel,
        out_shape=jax.ShapeDtypeStruct((GROUP * SLOTS * STEPS, PER_KV * HD), bf16),
        in_specs=[smem, smem, smem, vmem, any_space, any_space, any_space],
        out_specs=vmem,
        scratch_shapes=[
            pltpu.VMEM(prompt_kv.shape, bf16),
            pltpu.VMEM(queries.shape, bf16),
            pltpu.VMEM(new_kv.shape, bf16),
            pltpu.VMEM((PROMPTS * POS, 2048), f32),
            pltpu.VMEM((HEADS, PROMPTS * POS, 2 * HD), bf16),
            pltpu.VMEM((4, 2, PROMPTS * POS, 2 * HD), bf16),
            pltpu.VMEM((4, OWNERS, 16, HD), bf16),
            pltpu.VMEM((4, OWNERS, 16, HD), bf16),
            pltpu.VMEM((OWNERS * 8, 2 * PROMPTS * POS), bf16),
            pltpu.VMEM((256, 256), bf16),
            pltpu.VMEM((SLOTS, HD, 512), bf16),
            pltpu.VMEM((8, 512), f32),
            pltpu.VMEM((8, 512), f32),
            pltpu.VMEM((SLOTS, HD, 512), f32),
            pltpu.SemaphoreType.DMA((3,)),
            pltpu.SemaphoreType.DMA((7,)),
            pltpu.SemaphoreType.DMA((4,)),
            pltpu.SemaphoreType.DMA((4,)),
            pltpu.SemaphoreType.DMA((4,)),
        ],
        compiler_params=pltpu.CompilerParams(
            collective_id=0, has_side_effects=True, vmem_limit_bytes=32 << 20
        ),
        cost_estimate=pl.CostEstimate(flops=10**9, bytes_accessed=3 << 20, transcendentals=1 << 20),
    )(prompt_lengths, owner_prompts, owner_counts, owner_prompts, prompt_kv, queries, new_kv)
    return result.reshape(queries.shape)


def solution(mesh):
    return jax.shard_map(
        local,
        mesh=mesh,
        in_specs=(
            P(None, ("head", "batch"), None),
            P(),
            P(),
            P("batch"),
            P("batch", None, "head"),
            P("batch", None, "head"),
        ),
        out_specs=P("batch", None, "head"),
        check_vma=False,
    )
```

```python
import math

import jax
import jax.numpy as jnp
from jax import lax
from jax.experimental import pallas as pl
from jax.experimental.pallas import tpu as pltpu
from jax.sharding import PartitionSpec as P

HD = 128
GROUP = 16
STEPS = 4
PER_KV = 8
HEADS = 8
PROMPTS = 64
SLOTS = 2
OWNERS = 64
RUNS = 4
POS = 2
MESH = pl.DeviceIdType.MESH
LOWEST = -1e30
SCALE = math.log2(math.e) / math.sqrt(HD)


def iota(shape, dim):
    return lax.broadcasted_iota(jnp.int32, shape, dim)


def place():
    head, batch = lax.axis_index("head"), lax.axis_index("batch")
    return head // 2, head % 2, batch // 4, batch % 4


def device(run, core, yx, node):
    return (lax.rem(run + RUNS, RUNS) * 2 + core, yx * 4 + node)


def relay_of(hop):
    run, _, _, node = place()
    odd, upper = node % 2, node // 2 == 1
    if hop == 1:
        return jnp.where(upper, run + 1, run + 3), jnp.where(upper, odd, 2 + odd)
    if hop == 2:
        return jnp.where(upper, run + 3, run + 1), jnp.where(upper, 2 + odd, odd)
    return run + 2, jnp.where(upper, odd, 2 + odd)


def source_of(hop, run, node):
    odd, upper = node % 2, node // 2 == 1
    if hop == 0:
        return run + 0 * node, node
    if hop == 1:
        return jnp.where(upper, run + 1, run + 3), jnp.where(upper, odd, 2 + odd)
    if hop == 2:
        return jnp.where(upper, run + 1, run + 3), jnp.where(upper, 2 + odd, odd)
    return run + 2, jnp.where(upper, odd, 2 + odd)


def kernel(lengths_hbm, prompts_hbm, counts_hbm, kv_hbm, q_hbm, new_hbm, out_ref,
           lengths, prompts, counts, prompts_v, kv, q, new, wide, send, land, picked, got, pick, sort, qt, top, total, acc,
           in_sem, s1, r1, s2, r2):
    run, core, yx, node = place()
    me_head, me = lax.axis_index("head"), lax.axis_index("batch")

    pairs = ((kv_hbm, kv), (prompts_hbm, prompts_v), (prompts_hbm, prompts), (lengths_hbm, lengths),
             (counts_hbm, counts), (q_hbm, q), (new_hbm, new))
    loads = [pltpu.make_async_copy(a, b, in_sem.at[i]) for i, (a, b) in enumerate(pairs)]
    for load in loads:
        load.start()

    barrier = pltpu.get_barrier_semaphore()
    for hop in (3, 2, 1):
        their_run, their_node = source_of(hop, run, node)
        for k in (0, 1):
            pl.semaphore_signal(barrier, inc=1, device_id=device(their_run, k, yx, their_node), device_id_type=MESH)
    pl.semaphore_signal(barrier, inc=1, device_id=device(run, 1 - core, yx, node), device_id_type=MESH)

    @pl.loop(1, OWNERS)
    def _(i):
        pl.semaphore_signal(barrier, inc=1, device_id=(me_head, lax.rem(me + i, OWNERS)), device_id_type=MESH)

    loads[0].wait()
    for p in range(PROMPTS):
        wide[POS * p : POS * (p + 1), :] = kv[p].astype(jnp.float32)
    for h in range(HEADS):
        send[h] = wide[:, h * 256 : (h + 1) * 256].astype(jnp.bfloat16)

    rows, cols = OWNERS * 8, 2 * PROMPTS * POS
    owner_hot = (iota((rows, OWNERS), 0) // 8 == iota((rows, OWNERS), 1)).astype(jnp.bfloat16)
    loads[1].wait()
    ids = lax.dot_general(
        owner_hot, prompts_v[...].astype(jnp.float32).astype(jnp.bfloat16), (((1,), (1,)), ((), ())),
        preferred_element_type=jnp.float32)
    r1d = iota((rows, 1), 0)
    ids = jnp.where(r1d // 4 % 2 == 0, ids[:, 0:1], ids[:, 1:2]).astype(jnp.int32)
    want = (r1d // 2 % 2) * (PROMPTS * POS) + ids * POS + r1d % 2
    pick[...] = (want == iota((rows, cols), 1)).astype(jnp.bfloat16)

    pl.semaphore_wait(barrier, 7 + OWNERS - 1)

    own = pltpu.make_async_copy(send.at[me_head], land.at[0, core], r1.at[0])
    own.start()
    first = []
    first.append(pltpu.make_async_remote_copy(
        send.at[run * 2 + 1 - core], land.at[0, core], s1.at[0], r1.at[0],
        device_id=device(run, 1 - core, yx, node), device_id_type=MESH))
    for hop in (1, 2, 3):
        to_run, to_node = relay_of(hop)
        for k in (0, 1):
            to = device(to_run, k, yx, to_node)
            first.append(pltpu.make_async_remote_copy(
                send.at[to[0]], land.at[hop, core], s1.at[2 * hop - 1 + k], r1.at[hop], device_id=to, device_id_type=MESH))
    for copy in first:
        copy.start()

    def relay(g):
        pltpu.make_async_copy(land.at[g], land.at[g], r1.at[g]).wait()
        found = jnp.dot(pick[...], land[g].reshape(cols, 256), preferred_element_type=jnp.float32)
        keys, values = found[:, :HD].reshape(OWNERS, 8, HD), found[:, HD:].reshape(OWNERS, 8, HD)
        picked[g] = jnp.concatenate([keys, values], axis=1).astype(jnp.bfloat16)
        pltpu.make_async_copy(picked.at[g, me], got.at[g, me], r2.at[g]).start()

        @pl.loop(1, OWNERS)
        def _(i):
            to = lax.rem(me + i, OWNERS)
            pltpu.make_async_remote_copy(
                picked.at[g, to], got.at[g, me], s2.at[g], r2.at[g],
                device_id=(me_head, to), device_id_type=MESH).start()

    relay(0)

    for load in loads[2:]:
        load.wait()
    for g in range(GROUP * SLOTS):
        wide[STEPS * g : STEPS * (g + 1), :1024] = q[g].astype(jnp.float32)
        wide[STEPS * g : STEPS * (g + 1), 1024:1280] = new[g].astype(jnp.float32)
    side = 64
    rows = PER_KV * side
    for s in range(SLOTS):
        part = wide[side * s : side * (s + 1), :1024].astype(jnp.bfloat16)
        flat = jnp.concatenate([part[:, i * HD : (i + 1) * HD] for i in range(PER_KV)], axis=0)
        qt[s] = flat.astype(jnp.float32).T.astype(jnp.bfloat16)
        mine = wide[side * s : side * (s + 1), 1024:1280].astype(jnp.bfloat16)
        scores = jnp.dot(mine[:, :HD], qt[s], preferred_element_type=jnp.float32) * SCALE
        key, query = iota((side, rows), 0), iota((side, rows), 1) % side
        seen = (key // STEPS == query // STEPS) & (key % STEPS <= query % STEPS)
        scores = jnp.where(seen, scores, LOWEST)
        m = jnp.max(scores, axis=0, keepdims=True)
        e = jnp.where(seen, jnp.exp2(scores - m), 0.0)
        top[s : s + 1, :] = m
        total[s : s + 1, :] = jnp.sum(e, axis=0, keepdims=True)
        acc[s] = lax.dot_general(mine[:, HD:], e.astype(jnp.bfloat16), (((0,), (0,)), ((), ())), preferred_element_type=jnp.float32)

    r, c = iota((256, 256), 0), iota((256, 256), 1)
    sort[...] = (c == (r // 4 % 16) * 16 + (r // 64) * 4 + r % 4).astype(jnp.bfloat16)

    relay(1)
    relay(2)
    relay(3)

    def attend(g):
        pltpu.make_async_copy(got.at[g], got.at[g], r2.at[g]).wait()
        flat = got[g].reshape(OWNERS * 16, HD)
        blocks = [
            jnp.dot(sort[...], flat[256 * i : 256 * (i + 1)], preferred_element_type=jnp.float32).astype(jnp.bfloat16)
            for i in range(4)
        ]
        n = iota((256, rows), 0)
        relay_id = n // 4
        from_run, from_node = source_of(g, run, relay_id % 4)
        from_head = lax.rem(from_run + RUNS, RUNS) * 2 + n // 2 % 2
        position = (from_head * OWNERS + relay_id // 4 * 4 + from_node) * POS + n % 2
        for s in range(SLOTS):
            keys = jnp.concatenate([b[64 * s : 64 * (s + 1)] for b in blocks], axis=0)
            values = jnp.concatenate([b[128 + 64 * s : 128 + 64 * (s + 1)] for b in blocks], axis=0)
            scores = jnp.dot(keys, qt[s], preferred_element_type=jnp.float32) * SCALE
            scores = jnp.where(position < lengths[prompts[s, me]], scores, LOWEST)
            before = top[s : s + 1, :]
            m = jnp.maximum(before, jnp.max(scores, axis=0, keepdims=True))
            e = jnp.exp2(scores - m)
            fade = jnp.exp2(before - m)
            top[s : s + 1, :] = m
            total[s : s + 1, :] = total[s : s + 1, :] * fade + jnp.sum(e, axis=0, keepdims=True)
            acc[s] = acc[s] * fade + lax.dot_general(
                values, e.astype(jnp.bfloat16), (((0,), (0,)), ((), ())), preferred_element_type=jnp.float32)

    for g in range(4):
        attend(g)

    for s in range(SLOTS):
        live = s * GROUP < counts[0]
        result = jnp.where(live, acc[s] / total[s : s + 1, :], 0.0).T.astype(jnp.bfloat16)
        for i in range(PER_KV):
            out_ref[side * s : side * (s + 1), i * HD : (i + 1) * HD] = result[side * i : side * (i + 1)]

    for copy in first:
        copy.wait_send()
    for g in range(4):
        sent = picked.at[g, pl.ds(0, OWNERS - 1)]
        pltpu.make_async_copy(sent, sent, s2.at[g]).wait()


def local(prompt_kv, prompt_lengths, owner_prompts, owner_counts, queries, new_kv):
    hbm, vmem = pl.BlockSpec(memory_space=pltpu.HBM), pl.BlockSpec(memory_space=pltpu.VMEM)
    bf16, f32 = jnp.bfloat16, jnp.float32
    result = pl.pallas_call(
        kernel,
        out_shape=jax.ShapeDtypeStruct((GROUP * SLOTS * STEPS, PER_KV * HD), bf16),
        in_specs=[hbm] * 6,
        out_specs=vmem,
        scratch_shapes=[
            pltpu.SMEM(prompt_lengths.shape, jnp.int32),
            pltpu.SMEM((SLOTS, OWNERS), jnp.int32),
            pltpu.SMEM(owner_counts.shape, jnp.int32),
            pltpu.VMEM((SLOTS, OWNERS), jnp.int32),
            pltpu.VMEM(prompt_kv.shape, bf16),
            pltpu.VMEM(queries.shape, bf16),
            pltpu.VMEM(new_kv.shape, bf16),
            pltpu.VMEM((PROMPTS * POS, 2048), f32),
            pltpu.VMEM((HEADS, PROMPTS * POS, 2 * HD), bf16),
            pltpu.VMEM((4, 2, PROMPTS * POS, 2 * HD), bf16),
            pltpu.VMEM((4, OWNERS, 16, HD), bf16),
            pltpu.VMEM((4, OWNERS, 16, HD), bf16),
            pltpu.VMEM((OWNERS * 8, 2 * PROMPTS * POS), bf16),
            pltpu.VMEM((256, 256), bf16),
            pltpu.VMEM((SLOTS, HD, 512), bf16),
            pltpu.VMEM((8, 512), f32),
            pltpu.VMEM((8, 512), f32),
            pltpu.VMEM((SLOTS, HD, 512), f32),
            pltpu.SemaphoreType.DMA((7,)),
            pltpu.SemaphoreType.DMA((7,)),
            pltpu.SemaphoreType.DMA((4,)),
            pltpu.SemaphoreType.DMA((4,)),
            pltpu.SemaphoreType.DMA((4,)),
        ],
        compiler_params=pltpu.CompilerParams(
            collective_id=0, has_side_effects=True, vmem_limit_bytes=60 << 20
        ),
        cost_estimate=pl.CostEstimate(flops=10**9, bytes_accessed=3 << 20, transcendentals=1 << 20),
    )(prompt_lengths, owner_prompts.T, owner_counts, prompt_kv, queries, new_kv)
    return result.reshape(queries.shape)


def solution(mesh):
    return jax.shard_map(
        local,
        mesh=mesh,
        in_specs=(
            P(None, ("head", "batch"), None),
            P(),
            P(),
            P("batch"),
            P("batch", None, "head"),
            P("batch", None, "head"),
        ),
        out_specs=P("batch", None, "head"),
        check_vma=False,
    )
```

```python
import math

import jax
import jax.numpy as jnp
from jax import lax
from jax.experimental import pallas as pl
from jax.experimental.pallas import tpu as pltpu
from jax.sharding import PartitionSpec as P

HD = 128
GROUP = 16
STEPS = 4
PER_KV = 8
HEADS = 8
PROMPTS = 64
SLOTS = 2
OWNERS = 64
RUNS = 4
POS = 2
MESH = pl.DeviceIdType.MESH
LOWEST = -1e30
SCALE = math.log2(math.e) / math.sqrt(HD)


def iota(shape, dim):
    return lax.broadcasted_iota(jnp.int32, shape, dim)


def place():
    head, batch = lax.axis_index("head"), lax.axis_index("batch")
    return head // 2, head % 2, batch // 4, batch % 4


def device(run, core, yx, node):
    return (lax.rem(run + RUNS, RUNS) * 2 + core, yx * 4 + node)


def relay_of(hop):
    run, _, _, node = place()
    odd, upper = node % 2, node // 2 == 1
    if hop == 1:
        return jnp.where(upper, run + 1, run + 3), jnp.where(upper, odd, 2 + odd)
    if hop == 2:
        return jnp.where(upper, run + 3, run + 1), jnp.where(upper, 2 + odd, odd)
    return run + 2, jnp.where(upper, odd, 2 + odd)


def source_of(hop, run, node):
    odd, upper = node % 2, node // 2 == 1
    if hop == 0:
        return run + 0 * node, node
    if hop == 1:
        return jnp.where(upper, run + 1, run + 3), jnp.where(upper, odd, 2 + odd)
    if hop == 2:
        return jnp.where(upper, run + 1, run + 3), jnp.where(upper, 2 + odd, odd)
    return run + 2, jnp.where(upper, odd, 2 + odd)


def kernel(lengths_hbm, prompts_hbm, counts, kv_hbm, q_hbm, new_hbm, out_ref,
           lengths, prompts, prompts_v, kv, q, new, wide, send, land, picked, got, pick, sort, qt, top, total, acc,
           in_sem, s1, r1, s2, r2):
    run, core, yx, node = place()
    me_head, me = lax.axis_index("head"), lax.axis_index("batch")

    pairs = ((kv_hbm, kv), (prompts_hbm, prompts_v), (prompts_hbm, prompts), (lengths_hbm, lengths),
             (q_hbm, q), (new_hbm, new))
    loads = [pltpu.make_async_copy(a, b, in_sem.at[i]) for i, (a, b) in enumerate(pairs)]
    for load in loads:
        load.start()

    barrier = pltpu.get_barrier_semaphore()
    for hop in (3, 2, 1):
        their_run, their_node = source_of(hop, run, node)
        for k in (0, 1):
            pl.semaphore_signal(barrier, inc=1, device_id=device(their_run, k, yx, their_node), device_id_type=MESH)
    pl.semaphore_signal(barrier, inc=1, device_id=device(run, 1 - core, yx, node), device_id_type=MESH)

    @pl.loop(1, OWNERS)
    def _(i):
        pl.semaphore_signal(barrier, inc=1, device_id=(me_head, lax.rem(me + i, OWNERS)), device_id_type=MESH)

    loads[0].wait()
    for p in range(PROMPTS):
        wide[POS * p : POS * (p + 1), :] = kv[p].astype(jnp.float32)
    for h in range(HEADS):
        send[h] = wide[:, h * 256 : (h + 1) * 256].astype(jnp.bfloat16)

    rows, cols = OWNERS * 8, 2 * PROMPTS * POS
    owner_hot = (iota((rows, OWNERS), 0) // 8 == iota((rows, OWNERS), 1)).astype(jnp.bfloat16)
    loads[1].wait()
    ids = lax.dot_general(
        owner_hot, prompts_v[...].astype(jnp.float32).astype(jnp.bfloat16), (((1,), (1,)), ((), ())),
        preferred_element_type=jnp.float32)
    r1d = iota((rows, 1), 0)
    ids = jnp.where(r1d // 4 % 2 == 0, ids[:, 0:1], ids[:, 1:2]).astype(jnp.int32)
    want = (r1d // 2 % 2) * (PROMPTS * POS) + ids * POS + r1d % 2
    pick[...] = (want == iota((rows, cols), 1)).astype(jnp.bfloat16)

    pl.semaphore_wait(barrier, 7 + OWNERS - 1)

    own = pltpu.make_async_copy(send.at[me_head], land.at[0, core], r1.at[0])
    own.start()
    first = []
    first.append(pltpu.make_async_remote_copy(
        send.at[run * 2 + 1 - core], land.at[0, core], s1.at[0], r1.at[0],
        device_id=device(run, 1 - core, yx, node), device_id_type=MESH))
    for hop in (1, 2, 3):
        to_run, to_node = relay_of(hop)
        for k in (0, 1):
            to = device(to_run, lax.rem(core + k, 2), yx, to_node)
            first.append(pltpu.make_async_remote_copy(
                send.at[to[0]], land.at[hop, core], s1.at[2 * hop - 1 + k], r1.at[hop], device_id=to, device_id_type=MESH))
    for copy in first:
        copy.start()

    def relay(g):
        pltpu.make_async_copy(land.at[g], land.at[g], r1.at[g]).wait()
        found = jnp.dot(pick[...], land[g].reshape(cols, 256), preferred_element_type=jnp.float32)
        keys, values = found[:, :HD].reshape(OWNERS, 8, HD), found[:, HD:].reshape(OWNERS, 8, HD)
        picked[g] = jnp.concatenate([keys, values], axis=1).astype(jnp.bfloat16)
        pltpu.make_async_copy(picked.at[g, me], got.at[g, me], r2.at[g]).start()

        @pl.loop(1, OWNERS)
        def _(i):
            to = lax.rem(me + i, OWNERS)
            pltpu.make_async_remote_copy(
                picked.at[g, to], got.at[g, me], s2.at[g], r2.at[g],
                device_id=(me_head, to), device_id_type=MESH).start()

    relay(0)

    for load in loads[2:]:
        load.wait()
    for g in range(GROUP * SLOTS):
        wide[STEPS * g : STEPS * (g + 1), :1024] = q[g].astype(jnp.float32)
        wide[STEPS * g : STEPS * (g + 1), 1024:1280] = new[g].astype(jnp.float32)
    side = 64
    rows = PER_KV * side
    for s in range(SLOTS):
        part = wide[side * s : side * (s + 1), :1024].astype(jnp.bfloat16)
        flat = jnp.concatenate([part[:, i * HD : (i + 1) * HD] for i in range(PER_KV)], axis=0)
        qt[s] = flat.astype(jnp.float32).T.astype(jnp.bfloat16)
        mine = wide[side * s : side * (s + 1), 1024:1280].astype(jnp.bfloat16)
        scores = jnp.dot(mine[:, :HD], qt[s], preferred_element_type=jnp.float32) * SCALE
        key, query = iota((side, rows), 0), iota((side, rows), 1) % side
        seen = (key // STEPS == query // STEPS) & (key % STEPS <= query % STEPS)
        scores = jnp.where(seen, scores, LOWEST)
        m = jnp.max(scores, axis=0, keepdims=True)
        e = jnp.where(seen, jnp.exp2(scores - m), 0.0)
        top[s : s + 1, :] = m
        total[s : s + 1, :] = jnp.sum(e, axis=0, keepdims=True)
        acc[s] = lax.dot_general(mine[:, HD:], e.astype(jnp.bfloat16), (((0,), (0,)), ((), ())), preferred_element_type=jnp.float32)

    r, c = iota((256, 256), 0), iota((256, 256), 1)
    sort[...] = (c == (r // 4 % 16) * 16 + (r // 64) * 4 + r % 4).astype(jnp.bfloat16)

    relay(1)
    relay(2)
    relay(3)

    def attend(g):
        pltpu.make_async_copy(got.at[g], got.at[g], r2.at[g]).wait()
        flat = got[g].reshape(OWNERS * 16, HD)
        blocks = [
            jnp.dot(sort[...], flat[256 * i : 256 * (i + 1)], preferred_element_type=jnp.float32).astype(jnp.bfloat16)
            for i in range(4)
        ]
        n = iota((256, rows), 0)
        relay_id = n // 4
        from_run, from_node = source_of(g, run, relay_id % 4)
        from_head = lax.rem(from_run + RUNS, RUNS) * 2 + n // 2 % 2
        position = (from_head * OWNERS + relay_id // 4 * 4 + from_node) * POS + n % 2
        for s in range(SLOTS):
            keys = jnp.concatenate([b[64 * s : 64 * (s + 1)] for b in blocks], axis=0)
            values = jnp.concatenate([b[128 + 64 * s : 128 + 64 * (s + 1)] for b in blocks], axis=0)
            scores = jnp.dot(keys, qt[s], preferred_element_type=jnp.float32) * SCALE
            scores = jnp.where(position < lengths[prompts[s, me]], scores, LOWEST)
            before = top[s : s + 1, :]
            m = jnp.maximum(before, jnp.max(scores, axis=0, keepdims=True))
            e = jnp.exp2(scores - m)
            fade = jnp.exp2(before - m)
            top[s : s + 1, :] = m
            total[s : s + 1, :] = total[s : s + 1, :] * fade + jnp.sum(e, axis=0, keepdims=True)
            acc[s] = acc[s] * fade + lax.dot_general(
                values, e.astype(jnp.bfloat16), (((0,), (0,)), ((), ())), preferred_element_type=jnp.float32)

    for g in range(4):
        attend(g)

    for s in range(SLOTS):
        live = s * GROUP < counts[0]
        result = jnp.where(live, acc[s] / total[s : s + 1, :], 0.0).T.astype(jnp.bfloat16)
        for i in range(PER_KV):
            out_ref[side * s : side * (s + 1), i * HD : (i + 1) * HD] = result[side * i : side * (i + 1)]

    for copy in first:
        copy.wait_send()
    for g in range(4):
        sent = picked.at[g, pl.ds(0, OWNERS - 1)]
        pltpu.make_async_copy(sent, sent, s2.at[g]).wait()


def stay(x):
    return pltpu.with_memory_space_constraint(x, pltpu.HBM)


def local(prompt_kv, prompt_lengths, owner_prompts, owner_counts, queries, new_kv):
    hbm, vmem = pl.BlockSpec(memory_space=pltpu.HBM), pl.BlockSpec(memory_space=pltpu.VMEM)
    bf16, f32 = jnp.bfloat16, jnp.float32
    result = pl.pallas_call(
        kernel,
        out_shape=pltpu.VMEM((GROUP * SLOTS * STEPS, PER_KV * HD), bf16),
        in_specs=[hbm, hbm, pl.BlockSpec(memory_space=pltpu.SMEM), hbm, hbm, hbm],
        out_specs=vmem,
        scratch_shapes=[
            pltpu.SMEM(prompt_lengths.shape, jnp.int32),
            pltpu.SMEM((SLOTS, OWNERS), jnp.int32),
            pltpu.VMEM((SLOTS, OWNERS), jnp.int32),
            pltpu.VMEM(prompt_kv.shape, bf16),
            pltpu.VMEM(queries.shape, bf16),
            pltpu.VMEM(new_kv.shape, bf16),
            pltpu.VMEM((PROMPTS * POS, 2048), f32),
            pltpu.VMEM((HEADS, PROMPTS * POS, 2 * HD), bf16),
            pltpu.VMEM((4, 2, PROMPTS * POS, 2 * HD), bf16),
            pltpu.VMEM((4, OWNERS, 16, HD), bf16),
            pltpu.VMEM((4, OWNERS, 16, HD), bf16),
            pltpu.VMEM((OWNERS * 8, 2 * PROMPTS * POS), bf16),
            pltpu.VMEM((256, 256), bf16),
            pltpu.VMEM((SLOTS, HD, 512), bf16),
            pltpu.VMEM((8, 512), f32),
            pltpu.VMEM((8, 512), f32),
            pltpu.VMEM((SLOTS, HD, 512), f32),
            pltpu.SemaphoreType.DMA((6,)),
            pltpu.SemaphoreType.DMA((7,)),
            pltpu.SemaphoreType.DMA((4,)),
            pltpu.SemaphoreType.DMA((4,)),
            pltpu.SemaphoreType.DMA((4,)),
        ],
        compiler_params=pltpu.CompilerParams(
            collective_id=0, has_side_effects=True, vmem_limit_bytes=48 << 20
        ),
        cost_estimate=pl.CostEstimate(flops=10**9, bytes_accessed=3 << 20, transcendentals=1 << 20),
    )(stay(prompt_lengths), stay(owner_prompts.T), owner_counts, stay(prompt_kv), stay(queries), stay(new_kv))
    return result.reshape(queries.shape)


def solution(mesh):
    return jax.shard_map(
        local,
        mesh=mesh,
        in_specs=(
            P(None, ("head", "batch"), None),
            P(),
            P(),
            P("batch"),
            P("batch", None, "head"),
            P("batch", None, "head"),
        ),
        out_specs=P("batch", None, "head"),
        check_vma=False,
    )
```

```python
import math

import jax
import jax.numpy as jnp
from jax import lax
from jax.experimental import pallas as pl
from jax.experimental.pallas import tpu as pltpu
from jax.sharding import PartitionSpec as P

HD = 128
GROUP = 16
STEPS = 4
PER_KV = 8
HEADS = 8
PROMPTS = 64
SLOTS = 2
OWNERS = 64
RUNS = 4
POS = 2
MESH = pl.DeviceIdType.MESH
LOWEST = -1e30
SCALE = math.log2(math.e) / math.sqrt(HD)


def iota(shape, dim):
    return lax.broadcasted_iota(jnp.int32, shape, dim)


def place():
    head, batch = lax.axis_index("head"), lax.axis_index("batch")
    return head // 2, head % 2, batch // 4, batch % 4


def device(run, core, yx, node):
    return (lax.rem(run + RUNS, RUNS) * 2 + core, yx * 4 + node)


def relay_of(hop):
    run, _, _, node = place()
    odd, upper = node % 2, node // 2 == 1
    if hop == 1:
        return jnp.where(upper, run + 1, run + 3), jnp.where(upper, 0, 3), jnp.where(upper, 2 - odd, 1 + odd)
    if hop == 2:
        return jnp.where(upper, run + 3, run + 1), jnp.where(upper, 2, 1), jnp.where(upper, 1 + odd, 2 - odd)
    return run + 2, jnp.where(upper, odd, 2 + odd), 3


def source_of(group, run, node):
    if group == 0:
        return run + 0 * node, node
    if group == 3:
        return run + 2 + 0 * node, (node + 2) % 4
    left = node < 2
    return jnp.where(left, run + 3, run + 1), jnp.where(left, 4 - group, 5 + group) - 2 * node


def kernel(lengths_hbm, prompts_hbm, counts, kv_hbm, q_hbm, new_hbm, out_ref,
           lengths, prompts, prompts_v, kv, q, new, wide, send, land, picked, got, pick, sort, qt, top, total, acc,
           in_sem, s1, r1, s2, r2):
    run, core, yx, node = place()
    me_head, me = lax.axis_index("head"), lax.axis_index("batch")

    pairs = ((kv_hbm, kv), (prompts_hbm, prompts_v), (prompts_hbm, prompts), (lengths_hbm, lengths),
             (q_hbm, q), (new_hbm, new))
    loads = [pltpu.make_async_copy(a, b, in_sem.at[i]) for i, (a, b) in enumerate(pairs)]
    for load in loads:
        load.start()

    barrier = pltpu.get_barrier_semaphore()
    for group in (3, 2, 1):
        their_run, their_node = source_of(group, run, node)
        for k in (0, 1):
            pl.semaphore_signal(barrier, inc=1, device_id=device(their_run, k, yx, their_node), device_id_type=MESH)
    pl.semaphore_signal(barrier, inc=1, device_id=device(run, 1 - core, yx, node), device_id_type=MESH)

    @pl.loop(1, OWNERS)
    def _(i):
        pl.semaphore_signal(barrier, inc=1, device_id=(me_head, lax.rem(me + i, OWNERS)), device_id_type=MESH)

    loads[0].wait()
    for p in range(PROMPTS):
        wide[POS * p : POS * (p + 1), :] = kv[p].astype(jnp.float32)
    for h in range(HEADS):
        send[h] = wide[:, h * 256 : (h + 1) * 256].astype(jnp.bfloat16)

    rows, cols = OWNERS * 8, 2 * PROMPTS * POS
    owner_hot = (iota((rows, OWNERS), 0) // 8 == iota((rows, OWNERS), 1)).astype(jnp.bfloat16)
    loads[1].wait()
    ids = lax.dot_general(
        owner_hot, prompts_v[...].astype(jnp.float32).astype(jnp.bfloat16), (((1,), (1,)), ((), ())),
        preferred_element_type=jnp.float32)
    r1d = iota((rows, 1), 0)
    ids = jnp.where(r1d // 4 % 2 == 0, ids[:, 0:1], ids[:, 1:2]).astype(jnp.int32)
    want = (r1d // 2 % 2) * (PROMPTS * POS) + ids * POS + r1d % 2
    pick[...] = (want == iota((rows, cols), 1)).astype(jnp.bfloat16)

    pl.semaphore_wait(barrier, 7 + OWNERS - 1)

    own = pltpu.make_async_copy(send.at[me_head], land.at[0, core], r1.at[0])
    own.start()
    first = []
    first.append(pltpu.make_async_remote_copy(
        send.at[run * 2 + 1 - core], land.at[0, core], s1.at[0], r1.at[0],
        device_id=device(run, 1 - core, yx, node), device_id_type=MESH))
    for hop in (1, 2, 3):
        to_run, to_node, group = relay_of(hop)
        for k in (0, 1):
            to = device(to_run, lax.rem(core + k, 2), yx, to_node)
            first.append(pltpu.make_async_remote_copy(
                send.at[to[0]], land.at[group, core], s1.at[2 * hop - 1 + k], r1.at[group], device_id=to, device_id_type=MESH))
    for copy in first:
        copy.start()

    def relay(g):
        pltpu.make_async_copy(land.at[g], land.at[g], r1.at[g]).wait()
        found = jnp.dot(pick[...], land[g].reshape(cols, 256), preferred_element_type=jnp.float32)
        keys, values = found[:, :HD].reshape(OWNERS, 8, HD), found[:, HD:].reshape(OWNERS, 8, HD)
        picked[g] = jnp.concatenate([keys, values], axis=1).astype(jnp.bfloat16)
        pltpu.make_async_copy(picked.at[g, me], got.at[g, me], r2.at[g]).start()

        @pl.loop(1, OWNERS)
        def _(i):
            to = lax.rem(me + i, OWNERS)
            pltpu.make_async_remote_copy(
                picked.at[g, to], got.at[g, me], s2.at[g], r2.at[g],
                device_id=(me_head, to), device_id_type=MESH).start()

    relay(0)

    for load in loads[2:]:
        load.wait()
    for g in range(GROUP * SLOTS):
        wide[STEPS * g : STEPS * (g + 1), :1024] = q[g].astype(jnp.float32)
        wide[STEPS * g : STEPS * (g + 1), 1024:1280] = new[g].astype(jnp.float32)
    side = 64
    rows = PER_KV * side
    for s in range(SLOTS):
        part = wide[side * s : side * (s + 1), :1024].astype(jnp.bfloat16)
        flat = jnp.concatenate([part[:, i * HD : (i + 1) * HD] for i in range(PER_KV)], axis=0)
        qt[s] = flat.astype(jnp.float32).T.astype(jnp.bfloat16)
        mine = wide[side * s : side * (s + 1), 1024:1280].astype(jnp.bfloat16)
        scores = jnp.dot(mine[:, :HD], qt[s], preferred_element_type=jnp.float32) * SCALE
        key, query = iota((side, rows), 0), iota((side, rows), 1) % side
        seen = (key // STEPS == query // STEPS) & (key % STEPS <= query % STEPS)
        scores = jnp.where(seen, scores, LOWEST)
        m = jnp.max(scores, axis=0, keepdims=True)
        e = jnp.where(seen, jnp.exp2(scores - m), 0.0)
        top[s : s + 1, :] = m
        total[s : s + 1, :] = jnp.sum(e, axis=0, keepdims=True)
        acc[s] = lax.dot_general(mine[:, HD:], e.astype(jnp.bfloat16), (((0,), (0,)), ((), ())), preferred_element_type=jnp.float32)

    r, c = iota((256, 256), 0), iota((256, 256), 1)
    sort[...] = (c == (r // 4 % 16) * 16 + (r // 64) * 4 + r % 4).astype(jnp.bfloat16)

    relay(1)
    relay(2)
    relay(3)

    def attend(g):
        pltpu.make_async_copy(got.at[g], got.at[g], r2.at[g]).wait()
        flat = got[g].reshape(OWNERS * 16, HD)
        blocks = [
            jnp.dot(sort[...], flat[256 * i : 256 * (i + 1)], preferred_element_type=jnp.float32).astype(jnp.bfloat16)
            for i in range(4)
        ]
        n = iota((256, rows), 0)
        relay_id = n // 4
        from_run, from_node = source_of(g, run, relay_id % 4)
        from_head = lax.rem(from_run + RUNS, RUNS) * 2 + n // 2 % 2
        position = (from_head * OWNERS + relay_id // 4 * 4 + from_node) * POS + n % 2
        for s in range(SLOTS):
            keys = jnp.concatenate([b[64 * s : 64 * (s + 1)] for b in blocks], axis=0)
            values = jnp.concatenate([b[128 + 64 * s : 128 + 64 * (s + 1)] for b in blocks], axis=0)
            scores = jnp.dot(keys, qt[s], preferred_element_type=jnp.float32) * SCALE
            scores = jnp.where(position < lengths[prompts[s, me]], scores, LOWEST)
            before = top[s : s + 1, :]
            m = jnp.maximum(before, jnp.max(scores, axis=0, keepdims=True))
            e = jnp.exp2(scores - m)
            fade = jnp.exp2(before - m)
            top[s : s + 1, :] = m
            total[s : s + 1, :] = total[s : s + 1, :] * fade + jnp.sum(e, axis=0, keepdims=True)
            acc[s] = acc[s] * fade + lax.dot_general(
                values, e.astype(jnp.bfloat16), (((0,), (0,)), ((), ())), preferred_element_type=jnp.float32)

    for g in range(4):
        attend(g)

    for s in range(SLOTS):
        live = s * GROUP < counts[0]
        result = jnp.where(live, acc[s] / total[s : s + 1, :], 0.0).T.astype(jnp.bfloat16)
        for i in range(PER_KV):
            out_ref[side * s : side * (s + 1), i * HD : (i + 1) * HD] = result[side * i : side * (i + 1)]

    for copy in first:
        copy.wait_send()
    for g in range(4):
        sent = picked.at[g, pl.ds(0, OWNERS - 1)]
        pltpu.make_async_copy(sent, sent, s2.at[g]).wait()


def stay(x):
    return pltpu.with_memory_space_constraint(x, pltpu.HBM)


def local(prompt_kv, prompt_lengths, owner_prompts, owner_counts, queries, new_kv):
    hbm, vmem = pl.BlockSpec(memory_space=pltpu.HBM), pl.BlockSpec(memory_space=pltpu.VMEM)
    bf16, f32 = jnp.bfloat16, jnp.float32
    result = pl.pallas_call(
        kernel,
        out_shape=pltpu.VMEM((GROUP * SLOTS * STEPS, PER_KV * HD), bf16),
        in_specs=[hbm, hbm, pl.BlockSpec(memory_space=pltpu.SMEM), hbm, hbm, hbm],
        out_specs=vmem,
        scratch_shapes=[
            pltpu.SMEM(prompt_lengths.shape, jnp.int32),
            pltpu.SMEM((SLOTS, OWNERS), jnp.int32),
            pltpu.VMEM((SLOTS, OWNERS), jnp.int32),
            pltpu.VMEM(prompt_kv.shape, bf16),
            pltpu.VMEM(queries.shape, bf16),
            pltpu.VMEM(new_kv.shape, bf16),
            pltpu.VMEM((PROMPTS * POS, 2048), f32),
            pltpu.VMEM((HEADS, PROMPTS * POS, 2 * HD), bf16),
            pltpu.VMEM((4, 2, PROMPTS * POS, 2 * HD), bf16),
            pltpu.VMEM((4, OWNERS, 16, HD), bf16),
            pltpu.VMEM((4, OWNERS, 16, HD), bf16),
            pltpu.VMEM((OWNERS * 8, 2 * PROMPTS * POS), bf16),
            pltpu.VMEM((256, 256), bf16),
            pltpu.VMEM((SLOTS, HD, 512), bf16),
            pltpu.VMEM((8, 512), f32),
            pltpu.VMEM((8, 512), f32),
            pltpu.VMEM((SLOTS, HD, 512), f32),
            pltpu.SemaphoreType.DMA((6,)),
            pltpu.SemaphoreType.DMA((7,)),
            pltpu.SemaphoreType.DMA((4,)),
            pltpu.SemaphoreType.DMA((4,)),
            pltpu.SemaphoreType.DMA((4,)),
        ],
        compiler_params=pltpu.CompilerParams(
            collective_id=0, has_side_effects=True, vmem_limit_bytes=48 << 20
        ),
        cost_estimate=pl.CostEstimate(flops=10**9, bytes_accessed=3 << 20, transcendentals=1 << 20),
    )(stay(prompt_lengths), stay(owner_prompts.T), owner_counts, stay(prompt_kv), stay(queries), stay(new_kv))
    return result.reshape(queries.shape)


def solution(mesh):
    return jax.shard_map(
        local,
        mesh=mesh,
        in_specs=(
            P(None, ("head", "batch"), None),
            P(),
            P(),
            P("batch"),
            P("batch", None, "head"),
            P("batch", None, "head"),
        ),
        out_specs=P("batch", None, "head"),
        check_vma=False,
    )
```

```python
import math

import jax
import jax.numpy as jnp
from jax import lax
from jax.experimental import pallas as pl
from jax.experimental.pallas import tpu as pltpu
from jax.sharding import PartitionSpec as P

HD = 128
GROUP = 16
STEPS = 4
PER_KV = 8
HEADS = 8
PROMPTS = 64
SLOTS = 2
OWNERS = 64
RUNS = 4
POS = 2
MESH = pl.DeviceIdType.MESH
LOWEST = -1e30
SCALE = math.log2(math.e) / math.sqrt(HD)


def iota(shape, dim):
    return lax.broadcasted_iota(jnp.int32, shape, dim)


def place():
    head, batch = lax.axis_index("head"), lax.axis_index("batch")
    return head // 2, head % 2, batch // 4, batch % 4


def device(run, core, yx, node):
    return (lax.rem(run + RUNS, RUNS) * 2 + core, yx * 4 + node)


def relay_of(hop):
    run, _, _, node = place()
    odd, upper = node % 2, node // 2 == 1
    if hop == 1:
        return jnp.where(upper, run + 1, run + 3), jnp.where(upper, 0, 3), jnp.where(upper, 2 - odd, 1 + odd)
    if hop == 2:
        return jnp.where(upper, run + 3, run + 1), jnp.where(upper, 2, 1), jnp.where(upper, 1 + odd, 2 - odd)
    return run + 2, jnp.where(upper, odd, 2 + odd), 3


def source_of(group, run, node):
    if group == 0:
        return run + 0 * node, node
    if group == 3:
        return run + 2 + 0 * node, (node + 2) % 4
    left = node < 2
    return jnp.where(left, run + 3, run + 1), jnp.where(left, 4 - group, 5 + group) - 2 * node


def kernel(lengths_hbm, prompts_hbm, counts, kv_hbm, q_hbm, new_hbm, out_ref,
           lengths, prompts, prompts_v, kv, q, new, wide, send, land, picked, got, pick, sort, qt, top, total, acc,
           in_sem, s1, r1, s2, r2):
    run, core, yx, node = place()
    me_head, me = lax.axis_index("head"), lax.axis_index("batch")

    pairs = ((kv_hbm, kv), (prompts_hbm, prompts_v), (prompts_hbm, prompts), (lengths_hbm, lengths),
             (q_hbm, q), (new_hbm, new))
    loads = [pltpu.make_async_copy(a, b, in_sem.at[i]) for i, (a, b) in enumerate(pairs)]
    for load in loads:
        load.start()

    barrier = pltpu.get_barrier_semaphore()
    for group in (3, 2, 1):
        their_run, their_node = source_of(group, run, node)
        for k in (0, 1):
            pl.semaphore_signal(barrier, inc=1, device_id=device(their_run, k, yx, their_node), device_id_type=MESH)
    pl.semaphore_signal(barrier, inc=1, device_id=device(run, 1 - core, yx, node), device_id_type=MESH)

    @pl.loop(1, OWNERS)
    def _(i):
        pl.semaphore_signal(barrier, inc=1, device_id=(me_head, lax.rem(me + i, OWNERS)), device_id_type=MESH)

    loads[0].wait()
    for p in range(PROMPTS):
        wide[POS * p : POS * (p + 1), :] = kv[p].astype(jnp.float32)
    for h in range(HEADS):
        send[h] = wide[:, h * 256 : (h + 1) * 256].astype(jnp.bfloat16)

    rows, cols = OWNERS * 8, 2 * PROMPTS * POS
    owner_hot = (iota((rows, OWNERS), 0) // 8 == iota((rows, OWNERS), 1)).astype(jnp.bfloat16)
    loads[1].wait()
    ids = lax.dot_general(
        owner_hot, prompts_v[...].astype(jnp.float32).astype(jnp.bfloat16), (((1,), (1,)), ((), ())),
        preferred_element_type=jnp.float32)
    r1d = iota((rows, 1), 0)
    ids = jnp.where(r1d // 4 % 2 == 0, ids[:, 0:1], ids[:, 1:2]).astype(jnp.int32)
    want = (r1d // 2 % 2) * (PROMPTS * POS) + ids * POS + r1d % 2
    pick[...] = (want == iota((rows, cols), 1)).astype(jnp.bfloat16)

    pl.semaphore_wait(barrier, 7 + OWNERS - 1)

    own = pltpu.make_async_copy(send.at[me_head], land.at[0, core], r1.at[0])
    own.start()
    first = []
    first.append(pltpu.make_async_remote_copy(
        send.at[run * 2 + 1 - core], land.at[0, core], s1.at[0], r1.at[0],
        device_id=device(run, 1 - core, yx, node), device_id_type=MESH))
    for hop in (1, 2, 3):
        to_run, to_node, group = relay_of(hop)
        for k in (0, 1):
            to = device(to_run, lax.rem(core + k, 2), yx, to_node)
            first.append(pltpu.make_async_remote_copy(
                send.at[to[0]], land.at[group, core], s1.at[2 * hop - 1 + k], r1.at[group], device_id=to, device_id_type=MESH))
    for copy in first:
        copy.start()

    def relay(g):
        pltpu.make_async_copy(land.at[g], land.at[g], r1.at[g]).wait()
        found = jnp.dot(pick[...], land[g].reshape(cols, 256), preferred_element_type=jnp.float32)
        keys, values = found[:, :HD].reshape(OWNERS, 8, HD), found[:, HD:].reshape(OWNERS, 8, HD)
        picked[g] = jnp.concatenate([keys, values], axis=1).astype(jnp.bfloat16)
        pltpu.make_async_copy(picked.at[g, me], got.at[g, me], r2.at[g]).start()

        @pl.loop(1, OWNERS)
        def _(i):
            to = lax.rem(me + i, OWNERS)
            pltpu.make_async_remote_copy(
                picked.at[g, to], got.at[g, me], s2.at[g], r2.at[g],
                device_id=(me_head, to), device_id_type=MESH).start()

    relay(0)

    for load in loads[2:]:
        load.wait()
    for g in range(GROUP * SLOTS):
        wide[STEPS * g : STEPS * (g + 1), :1024] = q[g].astype(jnp.float32)
        wide[STEPS * g : STEPS * (g + 1), 1024:1280] = new[g].astype(jnp.float32)
    side = 64
    rows = PER_KV * side
    for s in range(SLOTS):
        part = wide[side * s : side * (s + 1), :1024].astype(jnp.bfloat16)
        flat = jnp.concatenate([part[:, i * HD : (i + 1) * HD] for i in range(PER_KV)], axis=0)
        qt[s] = flat.astype(jnp.float32).T.astype(jnp.bfloat16)
        mine = wide[side * s : side * (s + 1), 1024:1280].astype(jnp.bfloat16)
        scores = jnp.dot(mine[:, :HD], qt[s], preferred_element_type=jnp.float32) * SCALE
        key, query = iota((side, rows), 0), iota((side, rows), 1) % side
        seen = (key // STEPS == query // STEPS) & (key % STEPS <= query % STEPS)
        scores = jnp.where(seen, scores, LOWEST)
        m = jnp.max(scores, axis=0, keepdims=True)
        e = jnp.where(seen, jnp.exp2(scores - m), 0.0)
        top[s : s + 1, :] = m
        total[s : s + 1, :] = jnp.sum(e, axis=0, keepdims=True)
        acc[s] = lax.dot_general(mine[:, HD:], e.astype(jnp.bfloat16), (((0,), (0,)), ((), ())), preferred_element_type=jnp.float32)

    r, c = iota((256, 256), 0), iota((256, 256), 1)
    sort[...] = (c == (r // 4 % 16) * 16 + (r // 64) * 4 + r % 4).astype(jnp.bfloat16)

    relay(1)
    relay(2)
    relay(3)

    def attend(g):
        n = iota((256, 1), 0)
        relay_id = n // 4
        from_run, from_node = source_of(g, run, relay_id % 4)
        from_head = lax.rem(from_run + RUNS, RUNS) * 2 + n // 2 % 2
        position = (from_head * OWNERS + relay_id // 4 * 4 + from_node) * POS + n % 2
        inside = [position < lengths[prompts[s, me]] for s in range(SLOTS)]
        pltpu.make_async_copy(got.at[g], got.at[g], r2.at[g]).wait()
        flat = got[g].reshape(OWNERS * 16, HD)
        blocks = [
            jnp.dot(sort[...], flat[256 * i : 256 * (i + 1)], preferred_element_type=jnp.float32).astype(jnp.bfloat16)
            for i in range(4)
        ]
        for s in range(SLOTS):
            keys = jnp.concatenate([b[64 * s : 64 * (s + 1)] for b in blocks], axis=0)
            values = jnp.concatenate([b[128 + 64 * s : 128 + 64 * (s + 1)] for b in blocks], axis=0)
            scores = jnp.dot(keys, qt[s], preferred_element_type=jnp.float32) * SCALE
            scores = jnp.where(inside[s], scores, LOWEST)
            before = top[s : s + 1, :]
            m = jnp.maximum(before, jnp.max(scores, axis=0, keepdims=True))
            e = jnp.exp2(scores - m)
            fade = jnp.exp2(before - m)
            top[s : s + 1, :] = m
            total[s : s + 1, :] = total[s : s + 1, :] * fade + jnp.sum(e, axis=0, keepdims=True)
            acc[s] = acc[s] * fade + lax.dot_general(
                values, e.astype(jnp.bfloat16), (((0,), (0,)), ((), ())), preferred_element_type=jnp.float32)

    for g in range(4):
        attend(g)

    for s in range(SLOTS):
        live = s * GROUP < counts[0]
        result = (acc[s] * jnp.where(live, 1.0 / total[s : s + 1, :], 0.0)).T.astype(jnp.bfloat16)
        for i in range(PER_KV):
            out_ref[side * s : side * (s + 1), i * HD : (i + 1) * HD] = result[side * i : side * (i + 1)]

    for copy in first:
        copy.wait_send()
    for g in range(4):
        sent = picked.at[g, pl.ds(0, OWNERS - 1)]
        pltpu.make_async_copy(sent, sent, s2.at[g]).wait()


def stay(x):
    return pltpu.with_memory_space_constraint(x, pltpu.HBM)


def local(prompt_kv, prompt_lengths, owner_prompts, owner_counts, queries, new_kv):
    hbm, vmem = pl.BlockSpec(memory_space=pltpu.HBM), pl.BlockSpec(memory_space=pltpu.VMEM)
    bf16, f32 = jnp.bfloat16, jnp.float32
    result = pl.pallas_call(
        kernel,
        out_shape=pltpu.VMEM((GROUP * SLOTS * STEPS, PER_KV * HD), bf16),
        in_specs=[hbm, hbm, pl.BlockSpec(memory_space=pltpu.SMEM), hbm, hbm, hbm],
        out_specs=vmem,
        scratch_shapes=[
            pltpu.SMEM(prompt_lengths.shape, jnp.int32),
            pltpu.SMEM((SLOTS, OWNERS), jnp.int32),
            pltpu.VMEM((SLOTS, OWNERS), jnp.int32),
            pltpu.VMEM(prompt_kv.shape, bf16),
            pltpu.VMEM(queries.shape, bf16),
            pltpu.VMEM(new_kv.shape, bf16),
            pltpu.VMEM((PROMPTS * POS, 2048), f32),
            pltpu.VMEM((HEADS, PROMPTS * POS, 2 * HD), bf16),
            pltpu.VMEM((4, 2, PROMPTS * POS, 2 * HD), bf16),
            pltpu.VMEM((4, OWNERS, 16, HD), bf16),
            pltpu.VMEM((4, OWNERS, 16, HD), bf16),
            pltpu.VMEM((OWNERS * 8, 2 * PROMPTS * POS), bf16),
            pltpu.VMEM((256, 256), bf16),
            pltpu.VMEM((SLOTS, HD, 512), bf16),
            pltpu.VMEM((8, 512), f32),
            pltpu.VMEM((8, 512), f32),
            pltpu.VMEM((SLOTS, HD, 512), f32),
            pltpu.SemaphoreType.DMA((6,)),
            pltpu.SemaphoreType.DMA((7,)),
            pltpu.SemaphoreType.DMA((4,)),
            pltpu.SemaphoreType.DMA((4,)),
            pltpu.SemaphoreType.DMA((4,)),
        ],
        compiler_params=pltpu.CompilerParams(
            collective_id=0, has_side_effects=True, vmem_limit_bytes=48 << 20
        ),
        cost_estimate=pl.CostEstimate(flops=10**9, bytes_accessed=3 << 20, transcendentals=1 << 20),
    )(stay(prompt_lengths), stay(owner_prompts.T), owner_counts, stay(prompt_kv), stay(queries), stay(new_kv))
    return result.reshape(queries.shape)


def solution(mesh):
    return jax.shard_map(
        local,
        mesh=mesh,
        in_specs=(
            P(None, ("head", "batch"), None),
            P(),
            P(),
            P("batch"),
            P("batch", None, "head"),
            P("batch", None, "head"),
        ),
        out_specs=P("batch", None, "head"),
        check_vma=False,
    )
```
